32 devices in a mesh: grp: 2 (over x), ev: 4 (over y, core), hd: 4 (over z).
Axes of the slice: x: 2, y: 2, z: 4, core: 2. Of those that a mesh axis runs over, the one named last changes fastest.
Arguments:
- hist_keys: bfloat16 [8, 16384, 1024], P('grp', 'ev', 'hd'), parts along dimension 0, may hold values from -6 to 6
- hist_values: bfloat16 [8, 16384, 1024], P('grp', 'ev', 'hd'), parts along dimension 0, may hold values from -6 to 6
- hist_len: int32 [8], P('grp'), parts along dimension 0, may hold values from 4096 to 16384
- new_queries: bfloat16 [8, 1024, 1024], P('grp', 'ev', 'hd'), parts along dimension 0, may hold values from -6 to 6
- event_gate: bfloat16 [8, 1024, 1024], P('grp', 'ev', 'hd'), parts along dimension 0, may hold values from -6 to 6
- key_weight: bfloat16 [1024, 1024], P(None, 'hd'), may hold values from -0.1875 to 0.1875
- value_weight: bfloat16 [1024, 1024], P(None, 'hd'), may hold values from -0.1875 to 0.1875
- event_gain: float32 [1024], P('hd'), may hold values from 0.25 to 1.75
- cand_queries: bfloat16 [4096, 1024], P(('grp', 'ev'), 'hd'), parts along dimension 0, may hold values from -6 to 6
- cand_gate: bfloat16 [4096, 1024], P(('grp', 'ev'), 'hd'), parts along dimension 0, may hold values from -6 to 6
- cand_gain: float32 [1024], P('hd'), may hold values from 0.25 to 1.75
- block_user: int32 [32], P(('grp', 'ev')), parts along dimension 0, may hold values from 0 to 3, as said below
- cand_count: int32 [8], P('grp'), parts along dimension 0, may hold values from 1 to 1024, as said below
Outputs:
- event_out: bfloat16 [8, 1024, 1024], P('grp', 'ev', 'hd'), parts along dimension 0
- cand_out: bfloat16 [4096, 1024], P(('grp', 'ev'), 'hd'), parts along dimension 0
The draws below stay inside these ranges and needn't reach their ends.
There are 2 independent parts, one for each index of `grp`. The reference program is written for one: setup_inputs(seed, part) draws one part's arguments, and reference() takes and returns one part's arrays. A program takes and returns all parts, laid end to end along the dimension named above; an argument that names none is the same for every part. Nothing has to cross between parts.
Inputs may be any that keep to these rules, and one draw needn't show every extreme that they name: `block_user`: blocks belong to users in order: the first ceil(cand_count[0] / 128) blocks to user 0, the next ceil(cand_count[1] / 128) to user 1, and so on; every user has at least one block and all 16 blocks are used. `cand_count`: the blocks of users add up to 16 as stated for block_user; one user has exactly 8 full blocks.
All inputs are finite; a program needn't handle non-finite values.
Results may differ from the reference program's by a relative error of at most 0.0072.
Values may be sent and summed in bfloat16 or wider, within the bound.
A program may use at most 128 MiB of HBM per device.

```python
import jax
import jax.numpy as jnp
from jax import lax

USERS = 4
NEW = 1024
H = 8
HEAD = 128
D = 1024
HIST = 16384
BLOCK = 128
CANDS = 2048
NBLK = 16


def plan_blocks(key):
    busiest_blocks = NBLK // 2
    spare = NBLK - busiest_blocks - (USERS - 1)
    order = jax.random.permutation(jax.random.fold_in(key, 11), USERS).astype(jnp.int32)
    picks = jax.random.randint(jax.random.fold_in(key, 12), (spare,), 0, USERS - 1).astype(jnp.int32)
    owner = order[picks + 1]
    user_ids = jnp.arange(USERS, dtype=jnp.int32)
    is_busiest = (user_ids == order[0]).astype(jnp.int32)
    others = 1 + jnp.sum((owner[:, None] == user_ids[None, :]).astype(jnp.int32), axis=0)
    block_count = is_busiest * busiest_blocks + (1 - is_busiest) * others
    shortfall = jax.random.randint(jax.random.fold_in(key, 13), (USERS,), 0, BLOCK).astype(jnp.int32) * (1 - is_busiest)
    cand_total = (block_count * BLOCK - shortfall).astype(jnp.int32)
    ends = jnp.cumsum(block_count).astype(jnp.int32)
    block_ids = jnp.arange(NBLK, dtype=jnp.int32)
    block_owner = jnp.sum((block_ids[:, None] >= ends[None, :]).astype(jnp.int32), axis=1)
    return (block_owner.astype(jnp.int32), cand_total)


def draw_block_user(key, part):
    return plan_blocks(key)[0]


def draw_cand_count(key, part):
    return plan_blocks(key)[1]


def touch_ends(drawn, stream_key, low, high):
    spot = [jax.random.randint(jax.random.fold_in(stream_key, axis), (), 0, length) for axis, length in enumerate(drawn.shape)]
    widest = drawn.shape.index(max(drawn.shape))
    next_to = spot[:widest] + [(spot[widest] + 1) % drawn.shape[widest]] + spot[widest + 1:]
    return drawn.at[tuple(spot)].set(low).at[tuple(next_to)].set(high)


def block_scale(key, shape, split, low, top_value):
    def one(axis_at, parts):
        heights = jax.random.uniform(jax.random.fold_in(jax.random.fold_in(key, 6), axis_at), (parts,), jnp.float32, low / len(split), top_value / len(split))
        return jnp.repeat(jnp.exp(heights), shape[axis_at] // parts).reshape((-1,) + (1,) * (len(shape) - axis_at - 1))

    level = one(*split[0])
    for cut in split[1:]:
        level = level * one(*cut)
    return level


def noise(own_key, dims, scale, most, cuts=(), kind=jnp.bfloat16):
    entries = jax.random.normal(own_key, dims, jnp.float32) * scale
    if len(cuts) > 0:
        entries = block_scale(own_key, dims, cuts, -0.22, 0.18) * entries
    return jnp.clip(entries, min=-most, max=most).astype(kind)


def setup_inputs(seed: int = 0, part: int = 0) -> dict:
    key_list = jax.random.split(jax.random.key(seed), 14)
    own_keys = jax.random.split(jax.random.fold_in(key_list[13], part), 14)
    hist_keys = noise(own_keys[0], (USERS, HIST, D), 1.0, 6.0, ((1, 4), (2, 4)))
    hist_values = noise(own_keys[1], (USERS, HIST, D), 1.0, 6.0, ((1, 4), (2, 4)))
    hist_len = touch_ends(jax.random.randint(own_keys[2], (USERS,), HIST // 4, HIST + 1), jax.random.fold_in(own_keys[2], 1), HIST // 4, HIST).astype(jnp.int32)
    new_queries = noise(own_keys[3], (USERS, NEW, D), 1.0, 6.0, ((1, 4), (2, 4)))
    event_gate = noise(own_keys[4], (USERS, NEW, D), 1.0, 6.0, ((1, 4), (2, 4)))
    key_weight = noise(key_list[5], (D, D), D ** -0.5, 0.1875, ((1, 4),))
    value_weight = noise(key_list[6], (D, D), D ** -0.5, 0.1875, ((1, 4),))
    event_gain = jnp.clip(1.0 + 0.15 * jax.random.normal(key_list[7], (D,), jnp.float32), 0.25, 1.75)
    cand_queries = noise(own_keys[8], (CANDS, D), 1.0, 6.0, ((0, 4), (1, 4)))
    cand_gate = noise(own_keys[9], (CANDS, D), 1.0, 6.0, ((0, 4), (1, 4)))
    cand_gain = jnp.clip(1.0 + 0.15 * jax.random.normal(key_list[10], (D,), jnp.float32), 0.25, 1.75)
    block_user = draw_block_user(jax.random.fold_in(jax.random.fold_in(key_list[13], part), 71), part)
    cand_count = draw_cand_count(jax.random.fold_in(jax.random.fold_in(key_list[13], part), 71), part)
    return dict(hist_keys=hist_keys, hist_values=hist_values, hist_len=hist_len, new_queries=new_queries, event_gate=event_gate, key_weight=key_weight, value_weight=value_weight, event_gain=event_gain, cand_queries=cand_queries, cand_gate=cand_gate, cand_gain=cand_gain, block_user=block_user, cand_count=cand_count)


EPSILON = 1e-05

def head_norm(values, gain):
    centre = lax.optimization_barrier(jnp.mean(values, axis=-1, keepdims=True))
    shifted = values - centre
    spread = lax.optimization_barrier(jnp.mean(shifted * shifted, axis=-1, keepdims=True))
    return shifted * lax.rsqrt(spread + EPSILON) * gain

def reference(hist_keys, hist_values, hist_len, new_queries, event_gate, key_weight, value_weight, event_gain, cand_queries, cand_gate, cand_gain, block_user, cand_count):
    score_scale = HEAD ** (-0.5)
    key_block = min(1024, HIST)
    n_blocks = HIST // key_block
    queries_f = new_queries.astype(jnp.float32).reshape(USERS, NEW, H, HEAD)
    keys_split = hist_keys.reshape(USERS, n_blocks, key_block, H, HEAD)
    values_split = hist_values.reshape(USERS, n_blocks, key_block, H, HEAD)

    def history_step(total, block_idx):
        keys_here = lax.dynamic_index_in_dim(keys_split, block_idx, 1, keepdims=False).astype(jnp.float32)
        values_here = lax.dynamic_index_in_dim(values_split, block_idx, 1, keepdims=False).astype(jnp.float32)
        scores = jnp.einsum('unhd,ukhd->uhnk', queries_f, keys_here) * score_scale
        position = block_idx * key_block + jnp.arange(key_block, dtype=jnp.int32)
        alive = (position[None, :] < hist_len[:, None]).astype(jnp.float32)
        weights = (jax.nn.silu(scores) * alive[:, None, None, :]).astype(jnp.bfloat16)
        weights = lax.optimization_barrier(weights).astype(jnp.float32)
        return (total + jnp.einsum('uhnk,ukhd->unhd', weights, values_here), None)
    attended, _ = lax.scan(history_step, jnp.zeros((USERS, NEW, H, HEAD), jnp.float32), jnp.arange(n_blocks, dtype=jnp.int32))
    gate_e = event_gate.astype(jnp.float32).reshape(USERS, NEW, H, HEAD)
    event_out = (head_norm(attended, event_gain.reshape(H, HEAD)) * gate_e).astype(jnp.bfloat16).reshape(USERS, NEW, H * HEAD)
    flat = event_out.reshape(USERS * NEW, H * HEAD)
    fresh_keys = jnp.dot(flat, key_weight, preferred_element_type=jnp.float32).astype(jnp.bfloat16).reshape(USERS, NEW, H, HEAD)
    fresh_values = jnp.dot(flat, value_weight, preferred_element_type=jnp.float32).astype(jnp.bfloat16).reshape(USERS, NEW, H, HEAD)
    block_count = ((cand_count + BLOCK - 1) // BLOCK).astype(jnp.int32)
    first_block = jnp.cumsum(block_count).astype(jnp.int32) - block_count
    block_rank = jnp.arange(NBLK, dtype=jnp.int32) - first_block[block_user]
    limit = cand_count[block_user]
    cand_split = cand_queries.reshape(NBLK, BLOCK, H, HEAD)

    def candidate_block(items):
        block_query, owner = items
        keys_own = lax.dynamic_index_in_dim(fresh_keys, owner, 0, keepdims=False).astype(jnp.float32)
        values_own = lax.dynamic_index_in_dim(fresh_values, owner, 0, keepdims=False).astype(jnp.float32)
        scores = jnp.einsum('bhd,nhd->hbn', block_query.astype(jnp.float32), keys_own) * score_scale
        weights = jax.nn.silu(scores).astype(jnp.bfloat16)
        weights = lax.optimization_barrier(weights).astype(jnp.float32)
        return jnp.einsum('hbn,nhd->bhd', weights, values_own)
    cand_attn = lax.map(candidate_block, (cand_split, block_user))
    row_pos = block_rank[:, None] * BLOCK + jnp.arange(BLOCK, dtype=jnp.int32)[None, :]
    valid = (row_pos < limit[:, None]).astype(jnp.float32)
    gate_c = cand_gate.astype(jnp.float32).reshape(NBLK, BLOCK, H, HEAD)
    cand_out = (head_norm(cand_attn, cand_gain.reshape(H, HEAD)) * gate_c * valid[:, :, None, None]).astype(jnp.bfloat16).reshape(CANDS, H * HEAD)
    return (event_out, cand_out)
```

```python
import functools

import jax
import jax.numpy as jnp
from jax import lax
from jax.experimental import pallas as pl
from jax.experimental.pallas import tpu as pltpu
from jax.sharding import PartitionSpec as P

HEAD = 128
BLOCK = 128
EPSILON = 1e-05
HALF_SCALE = 0.5 * HEAD ** (-0.5)
F32 = jnp.float32
BF16 = jnp.bfloat16


def head_norm(values, gain):
    centre = jnp.mean(values, axis=-1, keepdims=True)
    shifted = values - centre
    spread = jnp.mean(shifted * shifted, axis=-1, keepdims=True)
    return shifted * lax.rsqrt(spread + EPSILON) * gain


def silu_weight(scores):
    half = (scores * HALF_SCALE).astype(BF16)
    return half * jnp.tanh(half) + half


def attend(q, k, v):
    scores = lax.dot_general(q, k, (((1,), (1,)), ((), ())), preferred_element_type=F32)
    return jnp.dot(silu_weight(scores), v, preferred_element_type=F32)


def kernel(
    n_ev,
    n_hd,
    hist_len,
    cand_count,
    keys_hbm,
    values_hbm,
    queries_hbm,
    egate_hbm,
    kw_hbm,
    vw_hbm,
    egain,
    candq_hbm,
    cgate_hbm,
    cgain,
    eout,
    cout,
    keys,
    values,
    queries,
    egate,
    kw,
    vw,
    candq,
    cgate,
    own_sum,
    pair_out,
    pair_in,
    cross_out,
    cross_in,
    everyone,
    fresh_k,
    fresh_v,
    cpair_out,
    cpair_in,
    ccross_out,
    ccross_in,
    own_cand,
    load_sem,
    misc_sem,
    q_send,
    q_recv,
    pair_send,
    pair_recv,
    cross_send,
    cross_recv,
    hd_send,
    hd_recv,
    cq_send,
    cq_recv,
    cp_send,
    cp_recv,
    cc_send,
    cc_recv,
):
    n_users, hist_rows, width = keys.shape
    n_heads = width // HEAD
    rows = queries.shape[2]
    cand_rows = candq.shape[1]
    n_blocks = cand_rows // BLOCK
    n_chips = n_ev // 2
    key_tile = min(1024, hist_rows)
    ev = lax.axis_index("ev")
    hd = lax.axis_index("hd")
    chip = ev // 2
    core = ev % 2
    partner = chip * 2 + (1 - core)

    def cols(head):
        return slice(head * HEAD, (head + 1) * HEAD)

    def remote(src, dst, send, recv, **where):
        return pltpu.make_async_remote_copy(
            src_ref=src,
            dst_ref=dst,
            send_sem=send,
            recv_sem=recv,
            device_id=where,
            device_id_type=pl.DeviceIdType.MESH,
        )

    def load_keys(u):
        return pltpu.make_async_copy(keys_hbm.at[u], keys.at[u], load_sem.at[0, u])

    def load_values(u):
        return pltpu.make_async_copy(values_hbm.at[u], values.at[u], load_sem.at[1, u])

    def load_queries(u):
        return pltpu.make_async_copy(queries_hbm.at[u], queries.at[u, ev], load_sem.at[2, u])

    def load_gate(u):
        return pltpu.make_async_copy(egate_hbm.at[u], egate.at[u], load_sem.at[3, u])

    misc = [
        pltpu.make_async_copy(src, dst, misc_sem.at[i])
        for i, (src, dst) in enumerate(
            [
                (candq_hbm, candq.at[ev]),
                (kw_hbm, kw),
                (vw_hbm, vw),
                (cgate_hbm, cgate),
            ]
        )
    ]

    def q_copy(u, step, owner):
        return remote(
            queries_hbm.at[u],
            queries.at[u, owner],
            q_send.at[u, step],
            q_recv.at[u, owner],
            ev=(ev + step) % n_ev,
        )

    def cq_copy(step, owner):
        return remote(
            candq_hbm, candq.at[owner], cq_send.at[step], cq_recv.at[owner], ev=(ev + step) % n_ev
        )

    def pair_copy(u, d):
        return remote(
            pair_out.at[u, d], pair_in.at[u, d], pair_send.at[u, d], pair_recv.at[u, d], ev=partner
        )

    def cross_copy(u, d):
        return remote(
            cross_out.at[u, d],
            cross_in.at[u, d],
            cross_send.at[u, d],
            cross_recv.at[u, d],
            ev=((chip + d) % n_chips) * 2 + core,
        )

    def hd_copy(u, step, owner):
        return remote(
            everyone.at[u, owner],
            everyone.at[u, owner],
            hd_send.at[u, step],
            hd_recv.at[u, owner],
            hd=(hd + step) % n_hd,
        )

    def cpair_copy(d):
        return remote(cpair_out.at[d], cpair_in.at[d], cp_send.at[d], cp_recv.at[d], ev=partner)

    def ccross_copy(d):
        return remote(
            ccross_out.at[d],
            ccross_in.at[d],
            cc_send.at[d],
            cc_recv.at[d],
            ev=((chip + d) % n_chips) * 2 + core,
        )

    load_queries(0).start()
    load_keys(0).start()
    load_values(0).start()
    barrier = pltpu.get_barrier_semaphore()
    for step in range(1, n_ev):
        pl.semaphore_signal(
            barrier,
            inc=1,
            device_id={"ev": (ev + step) % n_ev},
            device_id_type=pl.DeviceIdType.MESH,
        )
    for step in range(1, n_hd):
        pl.semaphore_signal(
            barrier,
            inc=1,
            device_id={"hd": (hd + step) % n_hd},
            device_id_type=pl.DeviceIdType.MESH,
        )
    for u in range(1, n_users):
        load_queries(u).start()
        load_keys(u).start()
        load_values(u).start()
    for u in range(n_users):
        load_gate(u).start()
    for copy in misc:
        copy.start()
    pl.semaphore_wait(barrier, n_ev - 1 + n_hd - 1)
    for u in range(n_users):
        for step in range(1, n_ev):
            q_copy(u, step, ev).start()

    def history(u, owner):
        return [
            functools.reduce(
                lambda a, b: a + b,
                [
                    attend(
                        queries[u, owner, :, cols(head)],
                        keys[u, at : at + key_tile, cols(head)],
                        values[u, at : at + key_tile, cols(head)],
                    )
                    for at in range(0, hist_rows, key_tile)
                ],
            )
            for head in range(n_heads)
        ]

    def finish_event(u):
        load_gate(u).wait()
        for d in range(1, n_chips):
            cross_copy(u, d).wait_recv()
        for head in range(n_heads):
            total = own_sum[u, :, cols(head)]
            for d in range(1, n_chips):
                total = total + cross_in[u, d, :, cols(head)].astype(F32)
            gate = egate[u, :, cols(head)].astype(F32)
            result = (head_norm(total, egain[:, cols(head)]) * gate).astype(BF16)
            everyone[u, hd, :, cols(head)] = result
            eout[u, :, cols(head)] = result
        for step in range(1, n_hd):
            hd_copy(u, step, hd).start()

    def user_step(u, carry):
        load_keys(u).wait()
        load_values(u).wait()
        load_queries(u).wait()

        @pl.when(u == min(1, n_users - 1))
        def _():
            for step in range(1, n_ev):
                cq_copy(step, ev).start()

        live = hist_len[u] - ev * hist_rows
        for at in range(0, hist_rows, key_tile):
            spot = lax.broadcasted_iota(jnp.int32, (key_tile, HEAD), 0) + at
            mask = jnp.where(spot < live, 1.0, 0.0).astype(BF16)
            for head in range(n_heads):
                values[u, at : at + key_tile, cols(head)] = (
                    values[u, at : at + key_tile, cols(head)] * mask
                )

        def chip_step(k, carry):
            d = jnp.where(u == 0, k, n_chips - 1 - k)
            there = ((chip + d) % n_chips) * 2

            other = there + (1 - core)
            q_copy(u, 1, other).wait_recv()
            for head, part in enumerate(history(u, other)):
                pair_out[u, d, :, cols(head)] = part.astype(BF16)
            pair_copy(u, d).start()

            @pl.when(d > 0)
            def _():
                q_copy(u, 1, there + core).wait_recv()

            parts = history(u, there + core)
            pair_copy(u, d).wait_recv()
            sums = [
                part + pair_in[u, d, :, cols(head)].astype(F32)
                for head, part in enumerate(parts)
            ]

            @pl.when(d > 0)
            def _():
                for head, total in enumerate(sums):
                    cross_out[u, d, :, cols(head)] = total.astype(BF16)
                cross_copy(u, d).start()

            @pl.when(d == 0)
            def _():
                for head, total in enumerate(sums):
                    own_sum[u, :, cols(head)] = total

            @pl.when((k == 0) & (u > 0))
            def _():
                finish_event(u - 1)

            return carry

        lax.fori_loop(0, n_chips, chip_step, 0)
        return carry

    lax.fori_loop(0, n_users, user_step, 0)
    finish_event(n_users - 1)
    for copy in misc:
        copy.wait()

    def project(u, carry):
        for step in range(1, n_hd):
            hd_copy(u, 1, (hd + step) % n_hd).wait_recv()
        for weight, fresh in ((kw, fresh_k), (vw, fresh_v)):
            total = jnp.dot(everyone[u, 0], weight[0:width], preferred_element_type=F32)
            for src in range(1, n_hd):
                total = total + jnp.dot(
                    everyone[u, src],
                    weight[src * width : (src + 1) * width],
                    preferred_element_type=F32,
                )
            fresh[u] = total.astype(BF16)
        return carry

    lax.fori_loop(0, n_users, project, 0)

    counts = [cand_count[u] for u in range(n_users)]
    ends = []
    for count in counts:
        blocks = (count + (BLOCK - 1)) // BLOCK
        ends.append(blocks if not ends else ends[-1] + blocks)

    def block_owner(block):
        owner = jnp.int32(0)
        for end in ends[:-1]:
            owner = owner + jnp.where(block >= end, 1, 0)
        return owner

    def candidates(dest):
        parts = []
        for i in range(n_blocks):
            owner = block_owner(dest * n_blocks + i)
            parts.append(
                [
                    attend(
                        candq[dest, i * BLOCK : (i + 1) * BLOCK, cols(head)],
                        fresh_k[owner, :, cols(head)],
                        fresh_v[owner, :, cols(head)],
                    )
                    for head in range(n_heads)
                ]
            )
        return parts

    for step in range(1, n_ev):
        cq_copy(1, (ev + step) % n_ev).wait_recv()

    def cand_step(k, carry):
        d = n_chips - 1 - k
        there = ((chip + d) % n_chips) * 2
        for i, parts in enumerate(candidates(there + (1 - core))):
            for head, part in enumerate(parts):
                cpair_out[d, i * BLOCK : (i + 1) * BLOCK, cols(head)] = part.astype(BF16)
        cpair_copy(d).start()
        mine = candidates(there + core)
        cpair_copy(d).wait_recv()
        sums = [
            [
                part + cpair_in[d, i * BLOCK : (i + 1) * BLOCK, cols(head)].astype(F32)
                for head, part in enumerate(parts)
            ]
            for i, parts in enumerate(mine)
        ]

        @pl.when(d > 0)
        def _():
            for i, parts in enumerate(sums):
                for head, total in enumerate(parts):
                    ccross_out[d, i * BLOCK : (i + 1) * BLOCK, cols(head)] = total.astype(BF16)
            ccross_copy(d).start()

        @pl.when(d == 0)
        def _():
            for i, parts in enumerate(sums):
                for head, total in enumerate(parts):
                    own_cand[i * BLOCK : (i + 1) * BLOCK, cols(head)] = total

        return carry

    lax.fori_loop(0, n_chips, cand_step, 0)

    for d in range(1, n_chips):
        ccross_copy(d).wait_recv()
    for i in range(n_blocks):
        block = ev * n_blocks + i
        owner = block_owner(block)
        first, limit = jnp.int32(0), counts[0]
        for u in range(1, n_users):
            first = jnp.where(owner >= u, ends[u - 1], first)
            limit = jnp.where(owner >= u, counts[u], limit)
        left = limit - (block - first) * BLOCK
        spot = lax.broadcasted_iota(jnp.int32, (BLOCK, HEAD), 0)
        mask = jnp.where(spot < left, 1.0, 0.0)
        span = slice(i * BLOCK, (i + 1) * BLOCK)
        for head in range(n_heads):
            total = own_cand[span, cols(head)]
            for d in range(1, n_chips):
                total = total + ccross_in[d, span, cols(head)].astype(F32)
            gate = cgate[span, cols(head)].astype(F32)
            cout[span, cols(head)] = (head_norm(total, cgain[:, cols(head)]) * gate * mask).astype(
                BF16
            )

    def drain(u, carry):
        for step in range(1, n_ev):
            q_copy(u, step, ev).wait_send()
        for d in range(n_chips):
            pair_copy(u, d).wait_send()
        for d in range(1, n_chips):
            cross_copy(u, d).wait_send()
        for step in range(1, n_hd):
            hd_copy(u, step, hd).wait_send()
        return carry

    lax.fori_loop(0, n_users, drain, 0)
    for step in range(1, n_ev):
        cq_copy(step, ev).wait_send()
    for d in range(n_chips):
        cpair_copy(d).wait_send()
    for d in range(1, n_chips):
        ccross_copy(d).wait_send()


def local(
    n_ev,
    n_hd,
    hist_keys,
    hist_values,
    hist_len,
    new_queries,
    event_gate,
    key_weight,
    value_weight,
    event_gain,
    cand_queries,
    cand_gate,
    cand_gain,
    block_user,
    cand_count,
):
    n_users, hist_rows, width = hist_keys.shape
    rows = new_queries.shape[1]
    cand_rows = cand_queries.shape[0]
    depth = key_weight.shape[0]
    n_chips = n_ev // 2
    dma = pltpu.SemaphoreType.DMA
    vmem, anywhere, smem = (
        pl.BlockSpec(memory_space=space) for space in (pltpu.VMEM, pl.ANY, pltpu.SMEM)
    )
    scratch = [
        pltpu.VMEM((n_users, hist_rows, width), BF16),
        pltpu.VMEM((n_users, hist_rows, width), BF16),
        pltpu.VMEM((n_users, n_ev, rows, width), BF16),
        pltpu.VMEM((n_users, rows, width), BF16),
        pltpu.VMEM((depth, width), BF16),
        pltpu.VMEM((depth, width), BF16),
        pltpu.VMEM((n_ev, cand_rows, width), BF16),
        pltpu.VMEM((cand_rows, width), BF16),
        pltpu.VMEM((n_users, rows, width), F32),
        pltpu.VMEM((n_users, n_chips, rows, width), BF16),
        pltpu.VMEM((n_users, n_chips, rows, width), BF16),
        pltpu.VMEM((n_users, n_chips, rows, width), BF16),
        pltpu.VMEM((n_users, n_chips, rows, width), BF16),
        pltpu.VMEM((n_users, n_hd, rows, width), BF16),
        pltpu.VMEM((n_users, rows, width), BF16),
        pltpu.VMEM((n_users, rows, width), BF16),
        pltpu.VMEM((n_chips, cand_rows, width), BF16),
        pltpu.VMEM((n_chips, cand_rows, width), BF16),
        pltpu.VMEM((n_chips, cand_rows, width), BF16),
        pltpu.VMEM((n_chips, cand_rows, width), BF16),
        pltpu.VMEM((cand_rows, width), F32),
        dma((4, n_users)),
        dma((4,)),
        dma((n_users, n_ev)),
        dma((n_users, n_ev)),
        dma((n_users, n_chips)),
        dma((n_users, n_chips)),
        dma((n_users, n_chips)),
        dma((n_users, n_chips)),
        dma((n_users, n_hd)),
        dma((n_users, n_hd)),
        dma((n_ev,)),
        dma((n_ev,)),
        dma((n_chips,)),
        dma((n_chips,)),
        dma((n_chips,)),
        dma((n_chips,)),
    ]
    flops = 4 * n_users * rows * n_ev * hist_rows * width + 4 * n_users * rows * depth * width
    return pl.pallas_call(
        functools.partial(kernel, n_ev, n_hd),
        out_shape=(
            jax.ShapeDtypeStruct((n_users, rows, width), BF16),
            jax.ShapeDtypeStruct((cand_rows, width), BF16),
        ),
        in_specs=[smem, smem]
        + [anywhere] * 6
        + [vmem, anywhere, anywhere, vmem],
        out_specs=(vmem, vmem),
        scratch_shapes=scratch,
        cost_estimate=pl.CostEstimate(
            flops=flops,
            bytes_accessed=4 * n_users * hist_rows * width,
            transcendentals=n_users * rows * n_ev * hist_rows * (width // HEAD),
        ),
        compiler_params=pltpu.CompilerParams(
            collective_id=0, has_side_effects=True, vmem_limit_bytes=56 << 20
        ),
    )(
        hist_len,
        cand_count,
        hist_keys,
        hist_values,
        new_queries,
        event_gate,
        key_weight,
        value_weight,
        event_gain.reshape(1, width),
        cand_queries,
        cand_gate,
        cand_gain.reshape(1, width),
    )


def solution(mesh):
    return jax.shard_map(
        functools.partial(local, mesh.shape["ev"], mesh.shape["hd"]),
        mesh=mesh,
        in_specs=(
            P("grp", "ev", "hd"),
            P("grp", "ev", "hd"),
            P("grp"),
            P("grp", "ev", "hd"),
            P("grp", "ev", "hd"),
            P(None, "hd"),
            P(None, "hd"),
            P("hd"),
            P(("grp", "ev"), "hd"),
            P(("grp", "ev"), "hd"),
            P("hd"),
            P(("grp", "ev")),
            P("grp"),
        ),
        out_specs=(P("grp", "ev", "hd"), P(("grp", "ev"), "hd")),
        check_vma=False,
    )
```

```python
import functools

import jax
import jax.numpy as jnp
from jax import lax
from jax.experimental import pallas as pl
from jax.experimental.pallas import tpu as pltpu
from jax.sharding import PartitionSpec as P

HEAD = 128
BLOCK = 128
EPSILON = 1e-05
HALF_SCALE = 0.5 * HEAD ** (-0.5)
F32 = jnp.float32
BF16 = jnp.bfloat16


def head_norm(values, gain):
    centre = jnp.mean(values, axis=-1, keepdims=True)
    shifted = values - centre
    spread = jnp.mean(shifted * shifted, axis=-1, keepdims=True)
    return shifted * lax.rsqrt(spread + EPSILON) * gain


def silu_weight(scores):
    half = (scores * HALF_SCALE).astype(BF16)
    return half * jnp.tanh(half) + half


def silu_wide(scores):
    half = scores * HALF_SCALE
    return (half * jnp.tanh(half) + half).astype(BF16)


def attend(q, k, v, silu=silu_weight):
    scores = lax.dot_general(q, k, (((1,), (1,)), ((), ())), preferred_element_type=F32)
    return jnp.dot(silu(scores), v, preferred_element_type=F32)


def kernel(
    n_ev,
    n_hd,
    hist_len,
    cand_count,
    keys_hbm,
    values_hbm,
    queries_hbm,
    egate_hbm,
    kw_hbm,
    vw_hbm,
    egain,
    candq_hbm,
    cgate_hbm,
    cgain,
    eout,
    cout,
    keys,
    values,
    queries,
    egate,
    kw,
    vw,
    candq,
    cgate,
    own_sum,
    pair_out,
    pair_in,
    cross_out,
    cross_in,
    everyone,
    fresh_k,
    fresh_v,
    cpair_out,
    cpair_in,
    ccross_out,
    ccross_in,
    own_cand,
    load_sem,
    misc_sem,
    q_send,
    q_recv,
    pair_send,
    pair_recv,
    cross_send,
    cross_recv,
    hd_send,
    hd_recv,
    cq_send,
    cq_recv,
    qf_send,
    cqf_send,
    cp_send,
    cp_recv,
    cc_send,
    cc_recv,
):
    n_users, hist_rows, width = keys.shape
    n_heads = width // HEAD
    rows = queries.shape[2]
    cand_rows = candq.shape[1]
    n_blocks = cand_rows // BLOCK
    n_chips = n_ev // 2
    key_tile = min(1024, hist_rows)
    ev = lax.axis_index("ev")
    hd = lax.axis_index("hd")
    chip = ev // 2
    core = ev % 2
    partner = chip * 2 + (1 - core)

    def cols(head):
        return slice(head * HEAD, (head + 1) * HEAD)

    def remote(src, dst, send, recv, **where):
        return pltpu.make_async_remote_copy(
            src_ref=src,
            dst_ref=dst,
            send_sem=send,
            recv_sem=recv,
            device_id=where,
            device_id_type=pl.DeviceIdType.MESH,
        )

    def load_keys(u):
        return pltpu.make_async_copy(keys_hbm.at[u], keys.at[u], load_sem.at[0, u])

    def load_values(u):
        return pltpu.make_async_copy(values_hbm.at[u], values.at[u], load_sem.at[1, u])

    def load_queries(u):
        return pltpu.make_async_copy(queries_hbm.at[u], queries.at[u, ev], load_sem.at[2, u])

    def load_gate(u):
        return pltpu.make_async_copy(egate_hbm.at[u], egate.at[u], load_sem.at[3, u])

    misc = [
        pltpu.make_async_copy(src, dst, misc_sem.at[i])
        for i, (src, dst) in enumerate(
            [
                (candq_hbm, candq.at[ev]),
                (kw_hbm, kw),
                (vw_hbm, vw),
                (cgate_hbm, cgate),
            ]
        )
    ]

    def device(d, flip):
        return ((chip + d) % n_chips) * 2 + (1 - core if flip else core)

    def q_copy(u, d, flip, owner):
        return remote(
            queries_hbm.at[u],
            queries.at[u, owner],
            q_send.at[u, 2 * d + flip],
            q_recv.at[u, owner],
            ev=device(d, flip),
        )

    def q_forward(u, d):
        owner = device(d, 0)
        return remote(
            queries.at[u, owner],
            queries.at[u, owner],
            qf_send.at[u, d],
            q_recv.at[u, owner],
            ev=partner,
        )

    def cq_copy(d, flip, owner):
        return remote(
            candq_hbm,
            candq.at[owner],
            cq_send.at[2 * d + flip],
            cq_recv.at[owner],
            ev=device(d, flip),
        )

    def cq_forward(d):
        owner = device(d, 0)
        return remote(
            candq.at[owner], candq.at[owner], cqf_send.at[d], cq_recv.at[owner], ev=partner
        )

    others = [(0, 1)] + [(d, flip) for d in range(1, n_chips) for flip in (0, 1)]
    firsts = [(0, 1)] + [(d, 0) for d in range(1, n_chips)]

    def pair_copy(u, d):
        return remote(
            pair_out.at[u, d], pair_in.at[u, d], pair_send.at[u, d], pair_recv.at[u, d], ev=partner
        )

    def cross_copy(u, d):
        return remote(
            cross_out.at[u, d],
            cross_in.at[u, d],
            cross_send.at[u, d],
            cross_recv.at[u, d],
            ev=((chip + d) % n_chips) * 2 + core,
        )

    def hd_copy(u, left, owner):
        return remote(
            everyone.at[u, owner],
            everyone.at[u, owner],
            hd_send.at[u, left, owner],
            hd_recv.at[u, owner],
            hd=hd - 1 if left else hd + 1,
        )

    def hd_pass(u, far, act):
        @pl.when((hd >= far) & (hd < n_hd - 1))
        def _():
            act(hd_copy(u, 0, hd - far))

        @pl.when((hd + far <= n_hd - 1) & (hd > 0))
        def _():
            act(hd_copy(u, 1, hd + far))

    def hd_hop(u, far):
        @pl.when(hd >= far)
        def _():
            hd_copy(u, 0, hd - far).wait_recv()

        @pl.when(hd + far <= n_hd - 1)
        def _():
            hd_copy(u, 0, hd + far).wait_recv()

        hd_pass(u, far, lambda copy: copy.start())

    def cpair_copy(d):
        return remote(cpair_out.at[d], cpair_in.at[d], cp_send.at[d], cp_recv.at[d], ev=partner)

    def ccross_copy(d):
        return remote(
            ccross_out.at[d],
            ccross_in.at[d],
            cc_send.at[d],
            cc_recv.at[d],
            ev=((chip + d) % n_chips) * 2 + core,
        )

    load_queries(0).start()
    load_keys(0).start()
    load_values(0).start()
    barrier = pltpu.get_barrier_semaphore()
    for step in range(1, n_ev):
        pl.semaphore_signal(
            barrier,
            inc=1,
            device_id={"ev": (ev + step) % n_ev},
            device_id_type=pl.DeviceIdType.MESH,
        )
    for step in range(1, n_hd):
        pl.semaphore_signal(
            barrier,
            inc=1,
            device_id={"hd": (hd + step) % n_hd},
            device_id_type=pl.DeviceIdType.MESH,
        )
    for u in range(1, n_users):
        load_queries(u).start()
        load_keys(u).start()
        load_values(u).start()
    for u in range(n_users):
        load_gate(u).start()
    for copy in misc:
        copy.start()
    pl.semaphore_wait(barrier, n_ev - 1 + n_hd - 1)
    for u in range(n_users):
        for d, flip in firsts if u else others:
            q_copy(u, d, flip, ev).start()

    def history(u, owner):
        return [
            functools.reduce(
                lambda a, b: a + b,
                [
                    attend(
                        queries[u, owner, :, cols(head)],
                        keys[u, at : at + key_tile, cols(head)],
                        values[u, at : at + key_tile, cols(head)],
                    )
                    for at in range(0, hist_rows, key_tile)
                ],
            )
            for head in range(n_heads)
        ]

    def finish_event(u):
        load_gate(u).wait()
        for d in range(1, n_chips):
            cross_copy(u, d).wait_recv()
        for head in range(n_heads):
            total = own_sum[u, :, cols(head)]
            for d in range(1, n_chips):
                total = total + cross_in[u, d, :, cols(head)].astype(F32)
            gate = egate[u, :, cols(head)].astype(F32)
            result = (head_norm(total, egain[:, cols(head)]) * gate).astype(BF16)
            everyone[u, hd, :, cols(head)] = result
            eout[u, :, cols(head)] = result
        hd_pass(u, 0, lambda copy: copy.start())

    def user_step(u, carry):
        load_keys(u).wait()
        load_values(u).wait()
        load_queries(u).wait()

        @pl.when(u == min(1, n_users - 1))
        def _():
            for d, flip in firsts:
                cq_copy(d, flip, ev).start()

        live = hist_len[u] - ev * hist_rows
        for at in range(0, hist_rows, key_tile):
            spot = lax.broadcasted_iota(jnp.int32, (key_tile, HEAD), 0) + at
            mask = jnp.where(spot < live, 1.0, 0.0).astype(BF16)
            for head in range(n_heads):
                values[u, at : at + key_tile, cols(head)] = (
                    values[u, at : at + key_tile, cols(head)] * mask
                )

        def chip_step(k, carry):
            d = jnp.where(u == 0, k, n_chips - 1 - k)
            there = ((chip + d) % n_chips) * 2

            other = there + (1 - core)
            q_copy(u, 0, 1, other).wait_recv()
            for head, part in enumerate(history(u, other)):
                pair_out[u, d, :, cols(head)] = part.astype(BF16)
            pair_copy(u, d).start()

            @pl.when((d > 0) & (u == 0))
            def _():
                q_copy(u, 0, 1, there + core).wait_recv()

            @pl.when((k == n_chips - 1) & (u < n_users - 1))
            def _():
                for far in range(1, n_chips):
                    q_copy(u + 1, 0, 1, device(far, 0)).wait_recv()
                    q_forward(u + 1, far).start()

            @pl.when((k == n_chips - 1) & (u == n_users - 1))
            def _():
                for far in range(1, n_chips):
                    cq_copy(0, 1, device(far, 0)).wait_recv()
                    cq_forward(far).start()

            @pl.when((k == n_chips - 1) & (u > 0))
            def _():
                hd_hop(u - 1, 1)

            parts = history(u, there + core)
            pair_copy(u, d).wait_recv()
            sums = [
                part + pair_in[u, d, :, cols(head)].astype(F32)
                for head, part in enumerate(parts)
            ]

            @pl.when(d > 0)
            def _():
                for head, total in enumerate(sums):
                    cross_out[u, d, :, cols(head)] = total.astype(BF16)
                cross_copy(u, d).start()

            @pl.when(d == 0)
            def _():
                for head, total in enumerate(sums):
                    own_sum[u, :, cols(head)] = total

            @pl.when((k == 0) & (u > 0))
            def _():
                finish_event(u - 1)

            @pl.when((k == n_chips - 1) & (u > 0))
            def _():
                for far in range(2, n_hd - 1):
                    hd_hop(u - 1, far)

            return carry

        lax.fori_loop(0, n_chips, chip_step, 0)
        return carry

    lax.fori_loop(0, n_users, user_step, 0)
    finish_event(n_users - 1)
    for copy in misc:
        copy.wait()

    def project(u):
        for weight, fresh in ((kw, fresh_k), (vw, fresh_v)):
            total = jnp.dot(everyone[u, 0], weight[0:width], preferred_element_type=F32)
            for src in range(1, n_hd):
                total = total + jnp.dot(
                    everyone[u, src],
                    weight[src * width : (src + 1) * width],
                    preferred_element_type=F32,
                )
            fresh[u] = total.astype(BF16)

    for u in range(max(n_users - 1, n_hd - 1)):
        if u < n_users - 1:
            if n_hd > 2:
                hd_hop(u, n_hd - 1)
            project(u)
        if u < n_hd - 1:
            hd_hop(n_users - 1, u + 1)
    project(n_users - 1)

    counts = [cand_count[u] for u in range(n_users)]
    ends = []
    for count in counts:
        blocks = (count + (BLOCK - 1)) // BLOCK
        ends.append(blocks if not ends else ends[-1] + blocks)

    def block_owner(block):
        owner = jnp.int32(0)
        for end in ends[:-1]:
            owner = owner + jnp.where(block >= end, 1, 0)
        return owner

    def candidates(dest):
        parts = []
        for i in range(n_blocks):
            owner = block_owner(dest * n_blocks + i)
            parts.append(
                [
                    attend(
                        candq[dest, i * BLOCK : (i + 1) * BLOCK, cols(head)],
                        fresh_k[owner, :, cols(head)],
                        fresh_v[owner, :, cols(head)],
                        silu_wide,
                    )
                    for head in range(n_heads)
                ]
            )
        return parts

    for d in range(n_chips):
        cq_copy(0, 1, device(d, 1)).wait_recv()

    def cand_step(k, carry):
        d = n_chips - 1 - k
        there = ((chip + d) % n_chips) * 2
        for i, parts in enumerate(candidates(there + (1 - core))):
            for head, part in enumerate(parts):
                cpair_out[d, i * BLOCK : (i + 1) * BLOCK, cols(head)] = part.astype(BF16)
        cpair_copy(d).start()
        mine = candidates(there + core)
        cpair_copy(d).wait_recv()
        sums = [
            [
                part + cpair_in[d, i * BLOCK : (i + 1) * BLOCK, cols(head)].astype(F32)
                for head, part in enumerate(parts)
            ]
            for i, parts in enumerate(mine)
        ]

        @pl.when(d > 0)
        def _():
            for i, parts in enumerate(sums):
                for head, total in enumerate(parts):
                    ccross_out[d, i * BLOCK : (i + 1) * BLOCK, cols(head)] = total.astype(BF16)
            ccross_copy(d).start()

        @pl.when(d == 0)
        def _():
            for i, parts in enumerate(sums):
                for head, total in enumerate(parts):
                    own_cand[i * BLOCK : (i + 1) * BLOCK, cols(head)] = total

        return carry

    lax.fori_loop(0, n_chips, cand_step, 0)

    for d in range(1, n_chips):
        ccross_copy(d).wait_recv()
    for i in range(n_blocks):
        block = ev * n_blocks + i
        owner = block_owner(block)
        first, limit = jnp.int32(0), counts[0]
        for u in range(1, n_users):
            first = jnp.where(owner >= u, ends[u - 1], first)
            limit = jnp.where(owner >= u, counts[u], limit)
        left = limit - (block - first) * BLOCK
        spot = lax.broadcasted_iota(jnp.int32, (BLOCK, HEAD), 0)
        mask = jnp.where(spot < left, 1.0, 0.0)
        span = slice(i * BLOCK, (i + 1) * BLOCK)
        for head in range(n_heads):
            total = own_cand[span, cols(head)]
            for d in range(1, n_chips):
                total = total + ccross_in[d, span, cols(head)].astype(F32)
            gate = cgate[span, cols(head)].astype(F32)
            cout[span, cols(head)] = (head_norm(total, cgain[:, cols(head)]) * gate * mask).astype(
                BF16
            )

    for u in range(n_users):
        for d, flip in firsts if u else others:
            q_copy(u, d, flip, ev).wait_send()
        for d in range(1, n_chips):
            if u:
                q_forward(u, d).wait_send()
            cross_copy(u, d).wait_send()
        for d in range(n_chips):
            pair_copy(u, d).wait_send()
        for far in range(n_hd - 1):
            hd_pass(u, far, lambda copy: copy.wait_send())
    for d, flip in firsts:
        cq_copy(d, flip, ev).wait_send()
    for d in range(1, n_chips):
        cq_forward(d).wait_send()
    for d in range(n_chips):
        cpair_copy(d).wait_send()
    for d in range(1, n_chips):
        ccross_copy(d).wait_send()


def local(
    n_ev,
    n_hd,
    hist_keys,
    hist_values,
    hist_len,
    new_queries,
    event_gate,
    key_weight,
    value_weight,
    event_gain,
    cand_queries,
    cand_gate,
    cand_gain,
    block_user,
    cand_count,
):
    n_users, hist_rows, width = hist_keys.shape
    rows = new_queries.shape[1]
    cand_rows = cand_queries.shape[0]
    depth = key_weight.shape[0]
    n_chips = n_ev // 2
    dma = pltpu.SemaphoreType.DMA
    vmem, anywhere, smem = (
        pl.BlockSpec(memory_space=space) for space in (pltpu.VMEM, pl.ANY, pltpu.SMEM)
    )
    scratch = [
        pltpu.VMEM((n_users, hist_rows, width), BF16),
        pltpu.VMEM((n_users, hist_rows, width), BF16),
        pltpu.VMEM((n_users, n_ev, rows, width), BF16),
        pltpu.VMEM((n_users, rows, width), BF16),
        pltpu.VMEM((depth, width), BF16),
        pltpu.VMEM((depth, width), BF16),
        pltpu.VMEM((n_ev, cand_rows, width), BF16),
        pltpu.VMEM((cand_rows, width), BF16),
        pltpu.VMEM((n_users, rows, width), F32),
        pltpu.VMEM((n_users, n_chips, rows, width), BF16),
        pltpu.VMEM((n_users, n_chips, rows, width), BF16),
        pltpu.VMEM((n_users, n_chips, rows, width), BF16),
        pltpu.VMEM((n_users, n_chips, rows, width), BF16),
        pltpu.VMEM((n_users, n_hd, rows, width), BF16),
        pltpu.VMEM((n_users, rows, width), BF16),
        pltpu.VMEM((n_users, rows, width), BF16),
        pltpu.VMEM((n_chips, cand_rows, width), BF16),
        pltpu.VMEM((n_chips, cand_rows, width), BF16),
        pltpu.VMEM((n_chips, cand_rows, width), BF16),
        pltpu.VMEM((n_chips, cand_rows, width), BF16),
        pltpu.VMEM((cand_rows, width), F32),
        dma((4, n_users)),
        dma((4,)),
        dma((n_users, n_ev)),
        dma((n_users, n_ev)),
        dma((n_users, n_chips)),
        dma((n_users, n_chips)),
        dma((n_users, n_chips)),
        dma((n_users, n_chips)),
        dma((n_users, 2, n_hd)),
        dma((n_users, n_hd)),
        dma((n_ev,)),
        dma((n_ev,)),
        dma((n_users, n_chips)),
        dma((n_chips,)),
        dma((n_chips,)),
        dma((n_chips,)),
        dma((n_chips,)),
        dma((n_chips,)),
    ]
    flops = 4 * n_users * rows * n_ev * hist_rows * width + 4 * n_users * rows * depth * width
    return pl.pallas_call(
        functools.partial(kernel, n_ev, n_hd),
        out_shape=(
            jax.ShapeDtypeStruct((n_users, rows, width), BF16),
            jax.ShapeDtypeStruct((cand_rows, width), BF16),
        ),
        in_specs=[smem, smem]
        + [anywhere] * 6
        + [vmem, anywhere, anywhere, vmem],
        out_specs=(vmem, vmem),
        scratch_shapes=scratch,
        cost_estimate=pl.CostEstimate(
            flops=flops,
            bytes_accessed=4 * n_users * hist_rows * width,
            transcendentals=n_users * rows * n_ev * hist_rows * (width // HEAD),
        ),
        compiler_params=pltpu.CompilerParams(
            collective_id=0, has_side_effects=True, vmem_limit_bytes=56 << 20
        ),
    )(
        hist_len,
        cand_count,
        hist_keys,
        hist_values,
        new_queries,
        event_gate,
        key_weight,
        value_weight,
        event_gain.reshape(1, width),
        cand_queries,
        cand_gate,
        cand_gain.reshape(1, width),
    )


def solution(mesh):
    return jax.shard_map(
        functools.partial(local, mesh.shape["ev"], mesh.shape["hd"]),
        mesh=mesh,
        in_specs=(
            P("grp", "ev", "hd"),
            P("grp", "ev", "hd"),
            P("grp"),
            P("grp", "ev", "hd"),
            P("grp", "ev", "hd"),
            P(None, "hd"),
            P(None, "hd"),
            P("hd"),
            P(("grp", "ev"), "hd"),
            P(("grp", "ev"), "hd"),
            P("hd"),
            P(("grp", "ev")),
            P("grp"),
        ),
        out_specs=(P("grp", "ev", "hd"), P(("grp", "ev"), "hd")),
        check_vma=False,
    )
```
